128 devices in a mesh: ctx: 128 (over z, x, y, core).
Axes of the slice: x: 4, y: 4, z: 4, core: 2. Of those that a mesh axis runs over, the one named last changes fastest.
Arguments:
- q_noised: bfloat16 [32768, 2048], P('ctx'), may hold values from -6 to 6
- k_noised: bfloat16 [32768, 2048], P('ctx'), may hold values from -6 to 6
- v_noised: bfloat16 [32768, 2048], P('ctx'), may hold values from -6 to 6
- dout: bfloat16 [32768, 2048], P('ctx'), may hold values from -6 to 6
- lse: float32 [16, 32768], P(None, 'ctx'), may hold values from 7.5 to 9
- delta: float32 [16, 32768], P(None, 'ctx'), may hold values from -48 to 48
- listed: int32 [128, 8], P('ctx'), may hold values from 0 to 255, as said below
- k_clean: bfloat16 [65536, 2048], P('ctx'), may hold values from -6 to 6
- v_clean: bfloat16 [65536, 2048], P('ctx'), may hold values from -6 to 6
Outputs:
- dq: bfloat16 [32768, 2048], P('ctx')
- dk_noised: bfloat16 [32768, 2048], P('ctx')
- dv_noised: bfloat16 [32768, 2048], P('ctx')
- dk_clean: bfloat16 [65536, 2048], P('ctx')
- dv_clean: bfloat16 [65536, 2048], P('ctx')
The draws below stay inside these ranges and needn't reach their ends.
Inputs may be any that keep to these rules, and one draw needn't show every extreme that they name: Row b lists 8 distinct clean blocks, each among the 16 clean blocks c with (b - 1 - c // 2) mod 128 < 8; how often a clean block is listed varies.
All inputs are finite; a program needn't handle non-finite values.
Results may differ from the reference program's by a relative error of at most 0.0053.
Values may be sent and summed in bfloat16 or wider, within the bound.
A program may use at most 384 MiB of HBM per device.

```python
import jax
import jax.numpy as jnp
from jax import lax

H = 16
HD = 128
BLOCK = 256
CLEAN_DEV = 2
LIST = 8
REACH = 8
NBLOCKS = 128
NOISED_TOK = 32768
CLEAN_TOK = 65536


def draw_listed(key, part):
    key = jax.random.fold_in(key, 11)
    key_pop, key_noise = jax.random.split(key)
    popular = jax.random.randint(key_pop, (CLEAN_DEV * NBLOCKS,), 1, 5)
    rows = jnp.arange(NBLOCKS, dtype=jnp.int32)[:, None]
    candidate = jnp.arange(REACH * CLEAN_DEV, dtype=jnp.int32)[None, :]
    owner = (rows - 1 - candidate // CLEAN_DEV) % NBLOCKS
    ids = owner * CLEAN_DEV + candidate % CLEAN_DEV
    noise = jax.random.randint(key_noise, (NBLOCKS, REACH * CLEAN_DEV), 0, 1000)
    score = noise * popular[ids] * 64 + candidate
    picked = lax.top_k(score, LIST)[1]
    return jnp.take_along_axis(ids, picked, axis=1).astype(jnp.int32)


def block_scale(key, shape, cuts, least, top_value):
    gain = 1.0
    for dim, blocks in cuts:
        steps = jax.random.uniform(jax.random.fold_in(jax.random.fold_in(key, 6), dim), (blocks,), jnp.float32, least / len(cuts), top_value / len(cuts))
        gain = gain * jnp.repeat(jnp.exp(steps), shape[dim] // blocks).reshape((-1,) + (1,) * (len(shape) - 1 - dim))
    return gain


def normal_values(stream_key, dims, deviation, most, shards=(), kind=jnp.bfloat16):
    drawn = deviation * jax.random.normal(stream_key, dims, jnp.float32)
    if shards:
        drawn = drawn * block_scale(stream_key, dims, shards, -0.22, 0.18)
    return jnp.clip(drawn, -most, most).astype(kind)


def setup_inputs(seed: int = 0) -> dict:
    arg_keys = jax.random.split(jax.random.key(seed), 10)
    q_noised = normal_values(arg_keys[0], (NOISED_TOK, H * HD), 1.0, 6.0, ((0, 128),))
    k_noised = normal_values(arg_keys[1], (NOISED_TOK, H * HD), 1.0, 6.0, ((0, 128),))
    v_noised = normal_values(arg_keys[2], (NOISED_TOK, H * HD), 1.0, 6.0, ((0, 128),))
    dout = normal_values(arg_keys[3], (NOISED_TOK, H * HD), 1.0, 6.0, ((0, 128),))
    lse = jnp.clip(7.5 + 1.5 * jax.random.uniform(arg_keys[4], (H, NOISED_TOK), jnp.float32) ** block_scale(arg_keys[4], (H, NOISED_TOK), ((1, 128),), -0.2, 0.2), 7.5, 9.0)
    delta = normal_values(arg_keys[5], (H, NOISED_TOK), 8.0, 48.0, ((1, 128),), jnp.float32)
    listed = draw_listed(jax.random.fold_in(arg_keys[9], 71), 0)
    k_clean = normal_values(arg_keys[7], (CLEAN_TOK, H * HD), 1.0, 6.0, ((0, 128),))
    v_clean = normal_values(arg_keys[8], (CLEAN_TOK, H * HD), 1.0, 6.0, ((0, 128),))
    return {"q_noised": q_noised, "k_noised": k_noised, "v_noised": v_noised, "dout": dout, "lse": lse, "delta": delta, "listed": listed, "k_clean": k_clean, "v_clean": v_clean}


def pair_grads(query, grad_out, log_sums, deltas, keys, values):
    rows = query.shape[0]
    scale = HD ** -0.5
    q_heads = query.reshape(rows, H, HD).astype(jnp.float32)
    o_heads = grad_out.reshape(rows, H, HD).astype(jnp.float32)
    k_heads = keys.reshape(keys.shape[0], H, HD).astype(jnp.float32)
    v_heads = values.reshape(values.shape[0], H, HD).astype(jnp.float32)
    scores = jnp.einsum("qhd,khd->hqk", q_heads, k_heads) * scale
    probs = jnp.exp(scores - log_sums[:, :, None])
    probs_low = lax.optimization_barrier(probs.astype(jnp.bfloat16)).astype(jnp.float32)
    grad_v = jnp.einsum("hqk,qhd->khd", probs_low, o_heads)
    grad_p = jnp.einsum("qhd,khd->hqk", o_heads, v_heads)
    grad_s = lax.optimization_barrier((probs * (grad_p - deltas[:, :, None])).astype(jnp.bfloat16)).astype(jnp.float32)
    grad_q = jnp.einsum("hqk,khd->qhd", grad_s, k_heads) * scale
    grad_k = jnp.einsum("hqk,qhd->khd", grad_s, q_heads) * scale
    width = H * HD
    return grad_q.reshape(rows, width), grad_k.reshape(keys.shape[0], width), grad_v.reshape(keys.shape[0], width)


def reference(q_noised, k_noised, v_noised, dout, lse, delta, listed, k_clean, v_clean):
    width = H * HD
    q_blocks = q_noised.reshape(NBLOCKS, BLOCK, width)
    k_blocks = k_noised.reshape(NBLOCKS, BLOCK, width)
    v_blocks = v_noised.reshape(NBLOCKS, BLOCK, width)
    o_blocks = dout.reshape(NBLOCKS, BLOCK, width)
    lse_blocks = lse.reshape(H, NBLOCKS, BLOCK).transpose(1, 0, 2)
    delta_blocks = delta.reshape(H, NBLOCKS, BLOCK).transpose(1, 0, 2)
    kc_blocks = k_clean.reshape(NBLOCKS * CLEAN_DEV, BLOCK, width)
    vc_blocks = v_clean.reshape(NBLOCKS * CLEAN_DEV, BLOCK, width)

    def one_block(carry, items):
        query, keys, values, grad_out, log_sums, deltas, ids = items
        grad_q, grad_k, grad_v = pair_grads(query, grad_out, log_sums, deltas, keys, values)

        def one_listed(inner, clean_id):
            acc_q, acc_k, acc_v = inner
            clean_id = clean_id.astype(jnp.int32)
            keys_c = lax.dynamic_index_in_dim(kc_blocks, clean_id, 0, keepdims=False)
            values_c = lax.dynamic_index_in_dim(vc_blocks, clean_id, 0, keepdims=False)
            part_q, part_k, part_v = pair_grads(query, grad_out, log_sums, deltas, keys_c, values_c)
            old_k = lax.dynamic_index_in_dim(acc_k, clean_id, 0, keepdims=False)
            old_v = lax.dynamic_index_in_dim(acc_v, clean_id, 0, keepdims=False)
            acc_k = lax.dynamic_update_index_in_dim(acc_k, old_k + part_k, clean_id, 0)
            acc_v = lax.dynamic_update_index_in_dim(acc_v, old_v + part_v, clean_id, 0)
            return (acc_q + part_q, acc_k, acc_v), None

        (grad_q, acc_k, acc_v), unused = lax.scan(one_listed, (grad_q, carry[0], carry[1]), ids)
        return (acc_k, acc_v), (grad_q.astype(jnp.bfloat16), grad_k.astype(jnp.bfloat16), grad_v.astype(jnp.bfloat16))

    start = jnp.zeros((NBLOCKS * CLEAN_DEV, BLOCK, width), jnp.float32)
    (acc_k, acc_v), (grad_q, grad_k, grad_v) = lax.scan(one_block, (start, start), (q_blocks, k_blocks, v_blocks, o_blocks, lse_blocks, delta_blocks, listed))
    return (grad_q.reshape(NOISED_TOK, width), grad_k.reshape(NOISED_TOK, width), grad_v.reshape(NOISED_TOK, width),
            acc_k.reshape(CLEAN_TOK, width).astype(jnp.bfloat16), acc_v.reshape(CLEAN_TOK, width).astype(jnp.bfloat16))
```

```python
import functools

import jax
import jax.numpy as jnp
from jax import lax
from jax.experimental import pallas as pl
from jax.experimental.pallas import tpu as pltpu
from jax.sharding import PartitionSpec as P

F32 = jnp.float32
BF16 = jnp.bfloat16
HD = 128
BLK = 256
CLEAN = 512
KEYS = 1024
RING = 4
SCALE = HD**-0.5
LOG2E = 1.4426950408889634
FAR_OFF = 1e30
STAT = 24

OWN, SAME, UP, DOWN, FAR = range(5)


def dot_nt(a, b):
    return lax.dot_general(a, b, (((1,), (1,)), ((), ())), preferred_element_type=F32)


def dot_nn(a, b):
    return lax.dot_general(a, b, (((1,), (0,)), ((), ())), preferred_element_type=F32)


def dot_tn(a, b):
    return lax.dot_general(a, b, (((0,), (0,)), ((), ())), preferred_element_type=F32)


def kernel(
    rows, nh,
    q, do, kn, vn, kc, vc, lse, delta, listed,
    dq, dkn, dvn, dkc, dvc,
    qd, kv, ms, st, mine, oq, near_p, same_p, ak, av, dkv, fs, fr, ns, nr, xs, xr, gs, gr, on, dqs,
    s_mine, s_loc, s_d2d, r_d2d, s_sd, r_sd,
    s_x, r_x, s_dn, r_dn, s_up, r_up, s_rd, s_ru, r_far,
    s_f, r_f, s_n, r_n, s_b, r_b, s_g, r_g, s_ol, s_or, r_or, s_on, s_dq,
):
    me = lax.axis_index("ctx")
    p = lax.rem(me, 2)
    j = lax.rem(me // 2, RING)
    r = me // (2 * RING)

    def dev(row, col, core):
        return row * (2 * RING) + col * 2 + core

    j_up, j_dn = lax.rem(j + 1, RING), lax.rem(j + RING - 1, RING)
    r_nx, r_pv = lax.rem(r + 1, rows), lax.rem(r + rows - 1, rows)
    sib = dev(r, j, 1 - p)
    up, dn, prev = dev(r, j_up, p), dev(r, j_dn, p), dev(r_pv, j, p)
    middle = jnp.logical_and(j >= 1, j <= 2)
    far_dir = jnp.where(j <= 1, 0, 1)
    far_to = jnp.where(j <= 1, up, dn)

    def remote(src, dst, ss, rs, to):
        return pltpu.make_async_remote_copy(
            src_ref=src, dst_ref=dst, send_sem=ss, recv_sem=rs,
            device_id=(to,), device_id_type=pl.DeviceIdType.MESH,
        )

    def cols(plane, g):
        return pl.ds(pl.multiple_of((plane * nh + g) * HD, HD), HD)

    my_rows = pl.ds(pl.multiple_of(p * CLEAN, CLEAN), CLEAN)
    other_rows = pl.ds(pl.multiple_of((1 - p) * CLEAN, CLEAN), CLEAN)

    def swap_places(g):
        return (
            (q, qd.at[OWN, g, p, 0]),
            (do, qd.at[OWN, g, p, 1]),
            (kc, kv.at[g, 0, my_rows]),
            (vc, kv.at[g, 1, my_rows]),
        )

    def swap_recv_places(g):
        return (
            (q, qd.at[OWN, g, 1 - p, 0]),
            (do, qd.at[OWN, g, 1 - p, 1]),
            (kc, kv.at[g, 0, other_rows]),
            (vc, kv.at[g, 1, other_rows]),
        )

    def swap_start(g):
        for n, (src, dst) in enumerate(swap_places(g)):
            remote(src.at[:, cols(1 - p, g)], dst, s_d2d.at[n, g], r_d2d.at[n, g], sib).start()
            pltpu.make_async_copy(src.at[:, cols(p, g)], dst, s_loc.at[n, g]).start()

    def swap_wait(g):
        for n, (src, dst) in enumerate(swap_places(g)):
            pltpu.make_async_copy(src.at[:, cols(p, g)], dst, s_loc.at[n, g]).wait()
        for n, (src, dst) in enumerate(swap_recv_places(g)):
            remote(src.at[:, cols(1 - p, g)], dst, s_d2d.at[n, g], r_d2d.at[n, g], sib).wait_recv()

    def swap_done(g):
        for n, (src, dst) in enumerate(swap_places(g)):
            remote(src.at[:, cols(1 - p, g)], dst, s_d2d.at[n, g], r_d2d.at[n, g], sib).wait_send()

    class Load:
        def __init__(self, ref, i, stats):
            self.i = i
            self.at = (lambda s: ref.at[s]) if stats else (lambda s: ref.at[s, i])
            self.blk = (lambda s, b: ref.at[s, b]) if stats else (lambda s, b: ref.at[s, i, b])

        def to_prev(self):
            return remote(self.at(OWN), self.at(SAME), s_x.at[self.i], r_x.at[self.i], prev)

        def down(self, slot):
            return remote(self.at(slot), self.at(UP), s_dn.at[self.i], r_dn.at[self.i], dn)

        def up(self, slot):
            return remote(self.at(slot), self.at(DOWN), s_up.at[self.i], r_up.at[self.i], up)

        def relay_down(self, b):
            return remote(
                self.blk(UP, b), self.blk(FAR, b), s_rd.at[b, self.i], r_far.at[b, self.i], dn
            )

        def relay_up(self, b):
            return remote(
                self.blk(DOWN, b), self.blk(FAR, b), s_ru.at[b, self.i], r_far.at[b, self.i], up
            )

        def send_own(self):
            self.to_prev().start()
            pl.when(j > 0)(lambda: self.down(OWN).start())
            pl.when(j == RING - 1)(lambda: self.up(OWN).start())

        def send_same(self):
            self.to_prev().wait_recv()
            pl.when(j == 0)(lambda: self.down(SAME).start())
            pl.when(j < RING - 1)(lambda: self.up(SAME).start())

        def relay(self):
            self.down(OWN).wait_recv()
            pl.when(j >= 1)(lambda: self.relay_down(0).start())
            pl.when(j == 1)(lambda: self.relay_down(1).start())
            self.up(OWN).wait_recv()
            pl.when(j <= 2)(lambda: self.relay_up(1).start())
            pl.when(j == 2)(lambda: self.relay_up(0).start())

        def far_wait(self):
            self.relay_down(0).wait_recv()
            self.relay_up(1).wait_recv()

        def done(self):
            self.to_prev().wait_send()
            self.down(OWN).wait_send()
            self.up(OWN).wait_send()
            pl.when(j >= 1)(lambda: self.relay_down(0).wait_send())
            pl.when(j == 1)(lambda: self.relay_down(1).wait_send())
            pl.when(j <= 2)(lambda: self.relay_up(1).wait_send())
            pl.when(j == 2)(lambda: self.relay_up(0).wait_send())

    def load(g):
        return Load(qd, g, False)

    stats = Load(st, nh, True)

    def far_copy(g):
        return remote(fs.at[g], fr.at[far_dir, g], s_f.at[g], r_f.at[far_dir, g], far_to)

    def far_recv(d, g):
        return remote(fs.at[g], fr.at[d, g], s_f.at[g], r_f.at[d, g], far_to)

    def near_copy(d, b, g):
        col = j_up if d == 0 else j_dn
        in_row = (j == RING - 1) if d == 0 else (j != 0)
        core = jnp.where(in_row, p, b)
        sub = jnp.where(in_row, b, p)
        return remote(
            ns.at[d, g, b], nr.at[d, g, sub], s_n.at[d, b, g], r_n.at[d, sub, g], dev(r, col, core)
        )

    def near_recv(d, b, g):
        return remote(ns.at[d, g, b], nr.at[d, g, b], s_n.at[d, b, g], r_n.at[d, b, g], up)

    def back_copy(b, g):
        return remote(xs.at[g, b], xr.at[g, p], s_b.at[b, g], r_b.at[p, g], dev(r_nx, j, b))

    def back_recv(b, g):
        return remote(xs.at[g, b], xr.at[g, b], s_b.at[b, g], r_b.at[b, g], dev(r_nx, j, b))

    def diag_copy(g):
        return remote(gs.at[g], gr.at[g], s_g.at[g], r_g.at[g], sib)

    def out_local(n, g):
        return pltpu.make_async_copy(
            dkv.at[g, n, my_rows], (dkc, dvc)[n].at[:, cols(p, g)], s_ol.at[n, g]
        )

    def out_remote(n, g):
        return remote(
            dkv.at[g, n, other_rows], (dkc, dvc)[n].at[:, cols(p, g)], s_or.at[n, g],
            r_or.at[n, g], sib,
        )

    def out_recv(n, g):
        return remote(
            dkv.at[g, n, other_rows], (dkc, dvc)[n].at[:, cols(1 - p, g)], s_or.at[n, g],
            r_or.at[n, g], sib,
        )

    def mine_copy(n):
        return pltpu.make_async_copy((q, do, kn, vn)[n], mine.at[n], s_mine.at[n])

    def noised_out(n):
        return pltpu.make_async_copy(on.at[n], (dkn, dvn)[n], s_on.at[n])

    def dq_out(plane, g):
        return pltpu.make_async_copy(dqs.at[:, cols(plane, g)], dq.at[:, cols(plane, g)], s_dq.at[plane, g])

    def grads(query, grad_out, keys, values, bias, deltas):
        s = dot_nt(keys, query)
        dp = dot_nt(values, grad_out)
        x = jnp.concatenate(
            [s[n * BLK : (n + 1) * BLK] * (SCALE * LOG2E) - row for n, row in enumerate(bias)], axis=0
        )
        prob = jnp.exp2(x)
        ds = (prob * (dp - deltas)).astype(BF16)
        return dot_tn(keys, ds), dot_nn(ds, query), dot_nn(prob.astype(BF16), grad_out)

    first_id = (me // 2) * 4

    def item(slot, b, g, c0, c1, first=False):
        ids = st[slot, b, 16:24, :]
        log_sums = st[slot, b, pl.ds(g, 1), :]
        bias = []
        for c in range(c0, c1):
            miss = jnp.min(jnp.abs(ids - (first_id + c).astype(F32)), axis=0, keepdims=True)
            bias.append(log_sums + jnp.minimum(miss, 1.0) * FAR_OFF)
        span = slice(c0 * BLK, c1 * BLK)
        d_q, d_k, d_v = grads(
            qd[slot, g, b, 0], qd[slot, g, b, 1], kv[g, 0, span], kv[g, 1, span],
            bias, st[slot, b, pl.ds(8 + g, 1), :],
        )
        if first:
            ak[span], av[span] = d_k, d_v
        else:
            ak[span] += d_k
            av[span] += d_v
        return d_q

    def own_pairs():
        for n in range(4):
            mine_copy(n).wait()

        def step(n, _):
            for h in (2 * n, 2 * n + 1):
                c = pl.ds(pl.multiple_of(h * HD, HD), HD)
                d_q, d_k, d_v = grads(
                    mine[0, :, c], mine[1, :, c], mine[2, :, c], mine[3, :, c],
                    [lse[pl.ds(h, 1), :] * LOG2E], delta[pl.ds(h, 1), :],
                )
                oq[h] = d_q
                on[0, :, c] = (d_k * SCALE).astype(BF16)
                on[1, :, c] = d_v.astype(BF16)
            return 0

        lax.fori_loop(0, nh, step, 0)
        for n in range(2):
            noised_out(n).start()

    def compute(g):
        odd = lax.rem(g, 2)
        near_p[0, odd, 0] = item(UP, 0, g, 0, 4, first=True)
        near_p[0, odd, 1] = item(UP, 1, g, 0, 4)
        diag = item(OWN, 1, g, 0, 2)

        @pl.when(p == 0)
        def _():
            gs[g] = diag.astype(BF16)
            diag_copy(g).start()

        @pl.when(p == 1)
        def _():
            oq[nh + g] += diag

        same_p[lax.rem(g, 4), 0] = item(SAME, 0, g, 0, 4)
        same_p[lax.rem(g, 4), 1] = item(SAME, 1, g, 2, 4)
        near_p[1, odd, 0] = item(DOWN, 0, g, 0, 4)
        near_p[1, odd, 1] = item(DOWN, 1, g, 0, 4)

    def compute_far(g):
        for b in range(2):
            fs[g, b] = item(FAR, b, g, 0, 4).astype(BF16)
        far_copy(g).start()
        dkv[g, 0] = (ak[...] * SCALE).astype(BF16)
        dkv[g, 1] = av[...].astype(BF16)
        for n in range(2):
            out_local(n, g).start()
            out_remote(n, g).start()

    def send_near(g):
        odd = lax.rem(g, 2)
        for d in range(2):

            @pl.when(middle)
            def _():
                far_recv(d, g).wait_recv()
                for b in range(2):
                    ns[d, g, b] = (near_p[d, odd, b] + fr[d, g, b].astype(F32)).astype(BF16)

            @pl.when(jnp.logical_not(middle))
            def _():
                for b in range(2):
                    ns[d, g, b] = near_p[d, odd, b].astype(BF16)

            for b in range(2):
                near_copy(d, b, g).start()

    def send_back(g):
        for d in range(2):
            for b in range(2):
                near_recv(d, b, g).wait_recv()
        for b in range(2):
            total = (
                same_p[lax.rem(g, 4), b]
                + jnp.where(j <= RING - 2, nr[1, g, b].astype(F32), 0.0)
                + jnp.where(j == 0, nr[0, g, b].astype(F32), 0.0)
            )
            xs[g, b] = total.astype(BF16)
            back_copy(b, g).start()

    def finish(g):
        @pl.when(p == 1)
        def _():
            diag_copy(g).wait_recv()
            oq[g] += gr[g].astype(F32)

        for plane in range(2):
            back_recv(plane, g).wait_recv()
            total = (
                oq[plane * nh + g]
                + xr[g, plane].astype(F32)
                + jnp.where(j >= 1, nr[0, g, plane].astype(F32), 0.0)
                + jnp.where(j == RING - 1, nr[1, g, plane].astype(F32), 0.0)
            )
            dqs[:, cols(plane, g)] = (total * SCALE).T.astype(BF16)
            dq_out(plane, g).start()

    for n in range(4):
        mine_copy(n).start()
    for plane in range(2):
        ms[plane, 0:nh] = lse[plane * nh : (plane + 1) * nh] * LOG2E
        ms[plane, 8 : 8 + nh] = delta[plane * nh : (plane + 1) * nh]
        for n in range(8):
            ms[plane, 16 + n : 17 + n] = jnp.full((1, BLK), listed[0, n].astype(F32))
    st[OWN, p] = ms[p]

    barrier = pltpu.get_barrier_semaphore()
    greeted = [sib] + [
        dev(a, b, c)
        for a, b in ((r, j_up), (r, j_dn), (r_nx, j), (r_pv, j))
        for c in range(2)
    ]
    for other in greeted:
        pl.semaphore_signal(
            barrier, inc=1, device_id=(other,), device_id_type=pl.DeviceIdType.MESH
        )
    pl.semaphore_wait(barrier, len(greeted))

    def stats_swap(blk):
        return remote(ms.at[1 - p], st.at[OWN, blk], s_sd.at[0], r_sd.at[0], sib)

    stats_swap(p).start()
    ahead = min(3, nh)
    for g in range(ahead):
        swap_start(g)
    stats_swap(1 - p).wait_recv()
    stats.send_own()
    for g in range(ahead):
        swap_wait(g)
        load(g).send_own()
    if ahead < nh:
        swap_start(ahead)
    stats.send_same()
    load(0).send_same()
    own_pairs()
    stats.relay()
    load(0).relay()
    if nh > 1:
        load(1).send_same()
    stats.far_wait()

    def step(t, _):
        @pl.when(t + 4 < nh)
        def _():
            swap_start(t + 4)

        @pl.when(t + 3 < nh)
        def _():
            swap_wait(t + 3)
            load(t + 3).send_own()

        @pl.when(t < nh)
        def _():
            compute(t)

        @pl.when(t + 2 < nh)
        def _():
            load(t + 2).send_same()

        @pl.when(t + 1 < nh)
        def _():
            load(t + 1).relay()

        @pl.when(t < nh)
        def _():
            load(t).far_wait()
            compute_far(t)

        @pl.when(jnp.logical_and(t >= 1, t < nh + 1))
        def _():
            send_near(t - 1)

        @pl.when(jnp.logical_and(t >= 2, t < nh + 2))
        def _():
            send_back(t - 2)

        @pl.when(t >= 3)
        def _():
            finish(t - 3)

        return 0

    lax.fori_loop(0, nh + 3, step, 0)

    stats_swap(p).wait_send()
    stats.done()
    for n in range(2):
        noised_out(n).wait()

    def drain(g, _):
        swap_done(g)
        load(g).done()
        far_copy(g).wait_send()
        for d in range(2):
            for b in range(2):
                near_copy(d, b, g).wait_send()
        for b in range(2):
            back_copy(b, g).wait_send()
            dq_out(b, g).wait()
            out_local(b, g).wait()
            out_remote(b, g).wait_send()
            out_recv(b, g).wait_recv()
        pl.when(p == 0)(lambda: diag_copy(g).wait_send())
        return 0

    lax.fori_loop(0, nh, drain, 0)


def per_device(rows, q_noised, k_noised, v_noised, dout, lse, delta, listed, k_clean, v_clean):
    width = q_noised.shape[1]
    nh = width // HD // 2
    vm, dma = pltpu.VMEM, pltpu.SemaphoreType.DMA
    hbm = pl.BlockSpec(memory_space=pl.ANY)
    tile = (HD, BLK)
    scratch = [
        vm((5, nh, 2, 2, BLK, HD), BF16),
        vm((nh, 2, KEYS, HD), BF16),
        vm((2, STAT, BLK), F32),
        vm((5, 2, STAT, BLK), F32),
        vm((4, BLK, width), BF16),
        vm((2 * nh, *tile), F32),
        vm((2, 2, 2, *tile), F32),
        vm((4, 2, *tile), F32),
        vm((KEYS, HD), F32),
        vm((KEYS, HD), F32),
        vm((nh, 2, KEYS, HD), BF16),
        vm((nh, 2, *tile), BF16),
        vm((2, nh, 2, *tile), BF16),
        vm((2, nh, 2, *tile), BF16),
        vm((2, nh, 2, *tile), BF16),
        vm((nh, 2, *tile), BF16),
        vm((nh, 2, *tile), BF16),
        vm((nh, *tile), BF16),
        vm((nh, *tile), BF16),
        vm((2, BLK, width), BF16),
        vm((BLK, width), BF16),
        dma((4,)),
        dma((4, nh)),
        dma((4, nh)),
        dma((4, nh)),
        dma((1,)),
        dma((1,)),
        *[dma((nh + 1,)) for _ in range(6)],
        dma((2, nh + 1)),
        dma((2, nh + 1)),
        dma((2, nh + 1)),
        dma((nh,)),
        dma((2, nh)),
        dma((2, 2, nh)),
        dma((2, 2, nh)),
        dma((2, nh)),
        dma((2, nh)),
        dma((nh,)),
        dma((nh,)),
        dma((2, nh)),
        dma((2, nh)),
        dma((2, nh)),
        dma((2,)),
        dma((2, nh)),
    ]
    pairs = 17 * 2 * nh
    return pl.pallas_call(
        functools.partial(kernel, rows, nh),
        out_shape=[jax.ShapeDtypeStruct((BLK, width), BF16)] * 3
        + [jax.ShapeDtypeStruct((CLEAN, width), BF16)] * 2,
        in_specs=[hbm] * 6
        + [pl.BlockSpec(memory_space=pltpu.VMEM)] * 2
        + [pl.BlockSpec(memory_space=pltpu.SMEM)],
        out_specs=[hbm] * 5,
        scratch_shapes=scratch,
        compiler_params=pltpu.CompilerParams(
            collective_id=0, has_side_effects=True, vmem_limit_bytes=60 * 2**20
        ),
        cost_estimate=pl.CostEstimate(
            flops=pairs * 10 * BLK * BLK * HD,
            bytes_accessed=15 * 2**20,
            transcendentals=pairs * BLK * BLK,
        ),
        name="block_attention_backward",
    )(q_noised, dout, k_noised, v_noised, k_clean, v_clean, lse, delta, listed)


def solution(mesh):
    rows = mesh.shape["ctx"] // (2 * RING)
    split = P("ctx", None)
    return jax.shard_map(
        functools.partial(per_device, rows),
        mesh=mesh,
        in_specs=(split,) * 4 + (P(None, "ctx"),) * 2 + (split,) * 3,
        out_specs=(split,) * 5,
        check_vma=False,
    )
```

```python
import functools

import jax
import jax.numpy as jnp
from jax import lax
from jax.experimental import pallas as pl
from jax.experimental.pallas import tpu as pltpu
from jax.sharding import PartitionSpec as P

F32 = jnp.float32
BF16 = jnp.bfloat16
HD = 128
BLK = 256
CLEAN = 512
RING = 4
SCALE = HD**-0.5
LOG2E = 1.4426950408889634
FAR_OFF = 1e30
STAT = 24

OWN, UP, DOWN, FAR = range(4)
HERE, BEFORE = range(2)


def dot_nt(a, b):
    return lax.dot_general(a, b, (((1,), (1,)), ((), ())), preferred_element_type=F32)


def dot_nn(a, b):
    return lax.dot_general(a, b, (((1,), (0,)), ((), ())), preferred_element_type=F32)


def dot_tn(a, b):
    return lax.dot_general(a, b, (((0,), (0,)), ((), ())), preferred_element_type=F32)


def kernel(
    rows, nh,
    q, do, kn, vn, kc, vc, lse, delta, listed,
    dq, dkn, dvn, dkc, dvc,
    qd, kv, lv, dv, ms, st, mine, oq, part, near_p, acc, db, dr, fs, fr, ns, nr, gs, gr, dqs,
    s_in, s_mine, s_loc, s_d2d, r_d2d, s_sd, r_sd, s_kb, r_kb,
    s_dn, r_dn, s_up, r_up, s_rd, s_ru, r_far,
    s_f, r_f, s_n, r_n, s_b, r_b, s_g, r_g, s_ol, s_or, r_or, s_on, s_dq,
):
    me = lax.axis_index("ctx")
    p = lax.rem(me, 2)
    j = lax.rem(me // 2, RING)
    r = me // (2 * RING)

    def dev(row, col, core):
        return row * (2 * RING) + col * 2 + core

    j_up, j_dn = lax.rem(j + 1, RING), lax.rem(j + RING - 1, RING)
    r_nx, r_pv = lax.rem(r + 1, rows), lax.rem(r + rows - 1, rows)
    sib = dev(r, j, 1 - p)
    up, dn, nxt, prev = dev(r, j_up, p), dev(r, j_dn, p), dev(r_nx, j, p), dev(r_pv, j, p)

    set_up = jnp.where(j < RING - 1, HERE, BEFORE)
    set_down = jnp.where(j > 0, BEFORE, HERE)
    set_far = jnp.where(j < RING // 2, HERE, BEFORE)

    def remote(src, dst, ss, rs, to):
        return pltpu.make_async_remote_copy(
            src_ref=src, dst_ref=dst, send_sem=ss, recv_sem=rs,
            device_id=(to,), device_id_type=pl.DeviceIdType.MESH,
        )

    def cols(plane, g):
        return pl.ds(pl.multiple_of((plane * nh + g) * HD, HD), HD)

    def swap_place(n, g, core):
        return qd.at[OWN, g, core, n] if n < 2 else kv.at[g, HERE, core, n - 2]

    def swap_local(n, g):
        return pltpu.make_async_copy(
            (q, do, kc, vc)[n].at[:, cols(p, g)], swap_place(n, g, p), s_loc.at[n, g]
        )

    def swap_send(n, g):
        return remote(
            (q, do, kc, vc)[n].at[:, cols(1 - p, g)], swap_place(n, g, p), s_d2d.at[n, g],
            r_d2d.at[n, g], sib,
        )

    def swap_recv(n, g):
        return remote(
            (q, do, kc, vc)[n].at[:, cols(1 - p, g)], swap_place(n, g, 1 - p), s_d2d.at[n, g],
            r_d2d.at[n, g], sib,
        )

    queries, clean = (0, 1), (2, 3)

    def swap_start(which, g):
        for n in which:
            swap_send(n, g).start()
        for n in which:
            swap_local(n, g).start()

    def swap_wait(which, g):
        for n in which:
            swap_local(n, g).wait()
            swap_recv(n, g).wait_recv()

    def keys_on(h, g):
        return remote(kv.at[g, HERE, h], kv.at[g, BEFORE, h], s_kb.at[h, g], r_kb.at[h, g], nxt)

    class Load:
        def __init__(self, ref, i, stats):
            self.i = i
            self.at = (lambda s: ref.at[s]) if stats else (lambda s: ref.at[s, i])
            self.blk = (lambda s, b: ref.at[s, b]) if stats else (lambda s, b: ref.at[s, i, b])

        def down(self):
            return remote(self.at(OWN), self.at(UP), s_dn.at[self.i], r_dn.at[self.i], dn)

        def up(self):
            return remote(self.at(OWN), self.at(DOWN), s_up.at[self.i], r_up.at[self.i], up)

        def relay_down(self):
            return remote(self.blk(UP, 0), self.blk(FAR, 0), s_rd.at[self.i], r_far.at[0, self.i], dn)

        def relay_up(self):
            return remote(self.blk(DOWN, 1), self.blk(FAR, 1), s_ru.at[self.i], r_far.at[1, self.i], up)

        def send_own(self):
            self.down().start()
            self.up().start()

        def relay(self):
            self.down().wait_recv()
            self.relay_down().start()
            self.up().wait_recv()
            self.relay_up().start()

        def far_wait(self):
            self.relay_down().wait_recv()
            self.relay_up().wait_recv()

        def done(self):
            self.down().wait_send()
            self.up().wait_send()
            self.relay_down().wait_send()
            self.relay_up().wait_send()

    def load(g):
        return Load(qd, g, False)

    stats = Load(st, nh, True)

    def far_copy(d, g):
        return remote(fs.at[d, g], fr.at[d, g], s_f.at[d, g], r_f.at[d, g], (up, dn)[d])

    def near_copy(d, b, g):
        return remote(
            ns.at[d, g, b], nr.at[d, g, p], s_n.at[d, b, g], r_n.at[d, p, g],
            dev(r, (j_up, j_dn)[d], b),
        )

    def near_recv(d, plane, g):
        return remote(
            ns.at[d, g, plane], nr.at[d, g, plane], s_n.at[d, plane, g], r_n.at[d, plane, g], up
        )

    def back_copy(h, g):
        return remote(db.at[g, h], dr.at[g, h], s_b.at[h, g], r_b.at[h, g], prev)

    def own_copy(g):
        return remote(gs.at[g], gr.at[g], s_g.at[g], r_g.at[g], sib)

    def out_local(n, g):
        return pltpu.make_async_copy(
            dr.at[g, p, n], (dkc, dvc)[n].at[:, cols(p, g)], s_ol.at[n, g]
        )

    def out_remote(n, g):
        return remote(
            dr.at[g, 1 - p, n], (dkc, dvc)[n].at[:, cols(p, g)], s_or.at[n, g], r_or.at[n, g], sib
        )

    def out_recv(n, g):
        return remote(
            dr.at[g, p, n], (dkc, dvc)[n].at[:, cols(1 - p, g)], s_or.at[n, g], r_or.at[n, g], sib
        )

    def mine_copy(n):
        return pltpu.make_async_copy((q, do, kn, vn)[n], mine.at[n], s_mine.at[n])

    def noised_out(n, plane, g):
        c = cols(plane, g)
        return pltpu.make_async_copy(
            mine.at[2 + n, :, c], (dkn, dvn)[n].at[:, c], s_on.at[n, plane, g]
        )

    def dq_out(plane, g):
        return pltpu.make_async_copy(
            dqs.at[:, cols(plane, g)], dq.at[:, cols(plane, g)], s_dq.at[plane, g]
        )

    def grads(query, grad_out, keys, values, bias, deltas):
        s = dot_nt(keys, query)
        dp = dot_nt(values, grad_out)
        x = jnp.concatenate(
            [s[n * BLK : (n + 1) * BLK] * (SCALE * LOG2E) - row for n, row in enumerate(bias)], axis=0
        )
        prob = jnp.exp2(x)
        ds = (prob * (dp - deltas)).astype(BF16)
        return dot_tn(keys, ds), dot_nn(ds, query), dot_nn(prob.astype(BF16), grad_out)

    first_here = (me // 2) * 4
    first_before = (r_pv * RING + j) * 4

    def item(slot, b, g, h, keys_set, first=False):
        first_id = jnp.where(keys_set == HERE, first_here, first_before) + 2 * h
        place = jnp.where(keys_set == HERE, lax.rem(2 * g + h, 4), 4)
        ids = st[slot, b, 16:24, :]
        log_sums = st[slot, b, pl.ds(g, 1), :]
        bias = []
        for c in range(2):
            miss = jnp.min(jnp.abs(ids - (first_id + c).astype(F32)), axis=0, keepdims=True)
            bias.append(log_sums + jnp.minimum(miss, 1.0) * FAR_OFF)
        d_q, d_k, d_v = grads(
            qd[slot, g, b, 0], qd[slot, g, b, 1], kv[g, keys_set, h, 0], kv[g, keys_set, h, 1],
            bias, st[slot, b, pl.ds(8 + g, 1), :],
        )
        if first:
            acc[place, 0], acc[place, 1] = d_k, d_v
        else:
            acc[place, 0] += d_k
            acc[place, 1] += d_v
        return d_q

    def own_pairs(g):
        for plane in range(2):
            h, c = plane * nh + g, cols(plane, g)
            d_q, d_k, d_v = grads(
                mine[0, :, c], mine[1, :, c], mine[2, :, c], mine[3, :, c],
                [lv[pl.ds(h, 1), :] * LOG2E], dv[pl.ds(h, 1), :],
            )
            oq[h] = d_q
            mine[2, :, c] = (d_k * SCALE).astype(BF16)
            mine[3, :, c] = d_v.astype(BF16)
        for n in range(2):
            for plane in range(2):
                noised_out(n, plane, g).start()

    def send_keys_grads(h, g):
        for n in range(2):
            db[g, h, n] = acc[4, n].astype(BF16)
        back_copy(h, g).start()

    def first_half(g):
        keys_on(0, g).wait_recv()

        @pl.when(g + 1 < nh)
        def _():
            swap_wait(clean, g + 1)
            keys_on(0, g + 1).start()

        part[OWN, 0] = item(OWN, 0, g, 0, BEFORE, first=True)
        part[OWN, 1] = item(OWN, 1, g, 0, HERE, first=True)
        for b in range(2):
            part[DOWN, b] = item(DOWN, b, g, 0, set_down)
        for b in range(2):
            part[UP, b] = item(UP, b, g, 0, set_up)

        @pl.when(g >= 1)
        def _():
            send_near(g - 1)

        @pl.when(g == 0)
        def _():
            stats.far_wait()

        load(g).far_wait()
        for b in range(2):
            part[FAR, b] = item(FAR, b, g, 0, set_far)
        send_keys_grads(0, g)

    def second_half(g):
        keys_on(1, g).wait_recv()

        @pl.when(g + 1 < nh)
        def _():
            keys_on(1, g + 1).start()

        for n in range(2):
            acc[lax.rem(2 * g + 1, 4), n] = jnp.zeros((CLEAN, HD), F32)
        own_0 = part[OWN, 0] + item(OWN, 0, g, 1, BEFORE, first=True)
        for b in range(2):
            fs[b, g] = (part[FAR, b] + item(FAR, b, g, 1, set_far)).astype(BF16)
        for d in range(2):
            far_copy(d, g).start()

        @pl.when(g + 2 < nh)
        def _():
            swap_wait(queries, g + 2)
            load(g + 2).send_own()

        own_1 = part[OWN, 1] + item(OWN, 1, g, 1, BEFORE)
        oq[p * nh + g] += jnp.where(p == 0, own_0, own_1)
        gs[g] = jnp.where(p == 0, own_1, own_0).astype(BF16)
        own_copy(g).start()
        ns[1, g, 0] = (part[DOWN, 0] + item(DOWN, 0, g, 1, set_down)).astype(BF16)
        near_copy(1, 0, g).start()
        near_p[1] = part[DOWN, 1] + item(DOWN, 1, g, 1, set_down)
        ns[0, g, 1] = (part[UP, 1] + item(UP, 1, g, 1, set_up)).astype(BF16)
        near_copy(0, 1, g).start()
        near_p[0] = part[UP, 0] + item(UP, 0, g, 1, set_up)
        send_keys_grads(1, g)

    def send_near(g):
        for d in range(2):
            far_copy(d, g).wait_recv()
            ns[d, g, d] = (near_p[d] + fr[d, g].astype(F32)).astype(BF16)
            near_copy(d, d, g).start()

    def finish_clean(h, g):
        back_copy(h, g).wait_recv()
        for n in range(2):
            total = acc[lax.rem(2 * g + h, 4), n] + dr[g, h, n].astype(F32)
            dr[g, h, n] = (total * (SCALE if n == 0 else 1.0)).astype(BF16)

        @pl.when(p == h)
        def _():
            for n in range(2):
                out_local(n, g).start()

        @pl.when(p != h)
        def _():
            for n in range(2):
                out_remote(n, g).start()

    def finish(g):
        own_copy(g).wait_recv()
        oq[(1 - p) * nh + g] += gr[g].astype(F32)
        for plane in range(2):
            for d in range(2):
                near_recv(d, plane, g).wait_recv()
            total = oq[plane * nh + g] + nr[0, g, plane].astype(F32) + nr[1, g, plane].astype(F32)
            dqs[:, cols(plane, g)] = (total * SCALE).T.astype(BF16)
            dq_out(plane, g).start()

    def drain(g):
        for n in range(4):
            swap_send(n, g).wait_send()
        load(g).done()
        own_copy(g).wait_send()
        for n in range(2):
            for m in range(2):
                near_copy(n, m, g).wait_send()
                noised_out(n, m, g).wait()
            keys_on(n, g).wait_send()
            far_copy(n, g).wait_send()
            back_copy(n, g).wait_send()
            dq_out(n, g).wait()
            out_local(n, g).wait()
            out_remote(n, g).wait_send()
            out_recv(n, g).wait_recv()

    barrier = pltpu.get_barrier_semaphore()
    greeted = [sib, nxt, prev] + [dev(r, col, core) for col in (j_up, j_dn) for core in range(2)]
    for other in greeted:
        pl.semaphore_signal(
            barrier, inc=1, device_id=(other,), device_id_type=pl.DeviceIdType.MESH
        )
    in_lse = pltpu.make_async_copy(lse, lv, s_in.at[0])
    in_delta = pltpu.make_async_copy(delta, dv, s_in.at[1])
    in_lse.start()
    in_delta.start()

    def stats_swap(blk):
        return remote(ms.at[1 - p], st.at[OWN, blk], s_sd.at[0], r_sd.at[0], sib)

    pl.semaphore_wait(barrier, len(greeted))
    swap_start(queries, 0)
    swap_start(clean, 0)
    in_lse.wait()
    in_delta.wait()
    for plane in range(2):
        ms[plane, 0:nh] = lv[plane * nh : (plane + 1) * nh] * LOG2E
        ms[plane, 8 : 8 + nh] = dv[plane * nh : (plane + 1) * nh]
        for n in range(8):
            ms[plane, 16 + n : 17 + n] = jnp.full((1, BLK), listed[0, n].astype(F32))
    st[OWN, p] = ms[p]
    stats_swap(p).start()
    swap_wait(queries, 0)
    load(0).send_own()
    swap_wait(clean, 0)
    keys_on(0, 0).start()
    stats_swap(1 - p).wait_recv()
    stats.send_own()
    for g in range(1, min(3, nh)):
        swap_start(queries, g)
    for g in range(1, min(2, nh)):
        swap_start(clean, g)
    for n in range(4):
        mine_copy(n).start()
    load(0).relay()
    stats.relay()
    keys_on(1, 0).start()
    if nh > 1:
        swap_wait(queries, 1)
        load(1).send_own()

    def step(t, _):
        @pl.when(t + 3 < nh)
        def _():
            swap_start(queries, t + 3)

        @pl.when(t + 2 < nh)
        def _():
            swap_start(clean, t + 2)

        first_half(t)

        @pl.when(t == 0)
        def _():
            for n in range(4):
                mine_copy(n).wait()

        own_pairs(t)

        @pl.when(t + 1 < nh)
        def _():
            load(t + 1).relay()

        second_half(t)

        @pl.when(t >= 1)
        def _():
            finish_clean(0, t - 1)
            finish_clean(1, t - 1)

        @pl.when(t >= 2)
        def _():
            finish(t - 2)

        @pl.when(t >= 3)
        def _():
            drain(t - 3)

        return 0

    lax.fori_loop(0, nh, step, 0)
    send_near(nh - 1)
    finish_clean(0, nh - 1)
    finish_clean(1, nh - 1)
    if nh > 1:
        finish(nh - 2)
    finish(nh - 1)

    stats_swap(p).wait_send()
    stats.done()
    for g in range(max(nh - 3, 0), nh):
        drain(g)


def copy_out(*refs):
    sources, results, held, arrive, leave = refs[:5], refs[5:10], refs[10:15], refs[15], refs[16]
    into, out = [], []
    for n in range(5):
        rows = sources[n].shape[0] // 2
        for k in range(2):
            span = pl.ds(k * rows, rows)
            into.append(pltpu.make_async_copy(sources[n].at[span], held[n].at[span], arrive.at[n, k]))
            out.append(pltpu.make_async_copy(held[n].at[span], results[n].at[span], leave.at[n, k]))
    for copy in into:
        copy.start()
    for one, two in zip(into, out, strict=True):
        one.wait()
        two.start()
    for copy in out:
        copy.wait()


def per_device(rows, q_noised, k_noised, v_noised, dout, lse, delta, listed, k_clean, v_clean):
    width = q_noised.shape[1]
    nh = width // HD // 2
    vm, dma = pltpu.VMEM, pltpu.SemaphoreType.DMA
    hbm = pl.BlockSpec(memory_space=pl.ANY)
    tile = (HD, BLK)
    scratch = [
        vm((4, nh, 2, 2, BLK, HD), BF16),
        vm((nh, 2, 2, 2, CLEAN, HD), BF16),
        vm((2 * nh, BLK), F32),
        vm((2 * nh, BLK), F32),
        vm((2, STAT, BLK), F32),
        vm((4, 2, STAT, BLK), F32),
        vm((4, BLK, width), BF16),
        vm((2 * nh, *tile), F32),
        vm((4, 2, *tile), F32),
        vm((2, *tile), F32),
        vm((5, 2, CLEAN, HD), F32),
        vm((nh, 2, 2, CLEAN, HD), BF16),
        vm((nh, 2, 2, CLEAN, HD), BF16),
        vm((2, nh, *tile), BF16),
        vm((2, nh, *tile), BF16),
        vm((2, nh, 2, *tile), BF16),
        vm((2, nh, 2, *tile), BF16),
        vm((nh, *tile), BF16),
        vm((nh, *tile), BF16),
        vm((BLK, width), BF16),
        dma((2,)),
        dma((4,)),
        dma((4, nh)),
        dma((4, nh)),
        dma((4, nh)),
        dma((1,)),
        dma((1,)),
        dma((2, nh)),
        dma((2, nh)),
        *[dma((nh + 1,)) for _ in range(6)],
        dma((2, nh + 1)),
        dma((2, nh)),
        dma((2, nh)),
        dma((2, 2, nh)),
        dma((2, 2, nh)),
        dma((2, nh)),
        dma((2, nh)),
        dma((nh,)),
        dma((nh,)),
        dma((2, nh)),
        dma((2, nh)),
        dma((2, nh)),
        dma((2, 2, nh)),
        dma((2, nh)),
    ]
    pairs = 17 * 2 * nh
    outs = pl.pallas_call(
        functools.partial(kernel, rows, nh),
        out_shape=[jax.ShapeDtypeStruct((BLK, width), BF16)] * 3
        + [jax.ShapeDtypeStruct((CLEAN, width), BF16)] * 2,
        in_specs=[hbm] * 8 + [pl.BlockSpec(memory_space=pltpu.SMEM)],
        out_specs=[hbm] * 5,
        scratch_shapes=scratch,
        compiler_params=pltpu.CompilerParams(
            collective_id=0, has_side_effects=True, vmem_limit_bytes=60 * 2**20
        ),
        cost_estimate=pl.CostEstimate(
            flops=pairs * 10 * BLK * BLK * HD,
            bytes_accessed=15 * 2**20,
            transcendentals=pairs * BLK * BLK,
        ),
        name="block_attention_backward",
    )(q_noised, dout, k_noised, v_noised, k_clean, v_clean, lse, delta, listed)
    return pl.pallas_call(
        copy_out,
        out_shape=[jax.ShapeDtypeStruct(out.shape, out.dtype) for out in outs],
        in_specs=[hbm] * 5,
        out_specs=[hbm] * 5,
        scratch_shapes=[vm(out.shape, out.dtype) for out in outs] + [dma((5, 2)), dma((5, 2))],
        name="copy_out",
    )(*outs)


def solution(mesh):
    rows = mesh.shape["ctx"] // (2 * RING)
    split = P("ctx", None)
    return jax.shard_map(
        functools.partial(per_device, rows),
        mesh=mesh,
        in_specs=(split,) * 4 + (P(None, "ctx"),) * 2 + (split,) * 3,
        out_specs=(split,) * 5,
        check_vma=False,
    )
```

```python
import functools

import jax
import jax.numpy as jnp
from jax import lax
from jax.experimental import pallas as pl
from jax.experimental.pallas import tpu as pltpu
from jax.sharding import PartitionSpec as P

F32 = jnp.float32
BF16 = jnp.bfloat16
HD = 128
BLK = 256
CLEAN = 512
RING = 4
SCALE = HD**-0.5
LOG2E = 1.4426950408889634
FAR_OFF = 1e30
STAT = 24

OWN, UP, DOWN, FAR = range(4)
HERE, BEFORE = range(2)


def dot_nt(a, b):
    return lax.dot_general(a, b, (((1,), (1,)), ((), ())), preferred_element_type=F32)


def dot_nn(a, b):
    return lax.dot_general(a, b, (((1,), (0,)), ((), ())), preferred_element_type=F32)


def dot_tn(a, b):
    return lax.dot_general(a, b, (((0,), (0,)), ((), ())), preferred_element_type=F32)


def kernel(
    rows, nh,
    q, do, kn, vn, kc, vc, lse, delta, listed,
    dq, dkn, dvn, dkc, dvc,
    qd, kv, lv, dv, ms, st, mine, oq, part, near_p, acc, db, dr, fs, fr, ns, nr, gs, gr, dqs,
    lm, s_in, s_mine, s_loc, s_d2d, r_d2d, s_sd, r_sd, s_kb, r_kb,
    s_q0, r_q0, s_k0, r_k0,
    s_dn, r_dn, s_up, r_up, s_rd, s_ru, r_far,
    s_f, r_f, s_n, r_n, s_b, r_b, s_g, r_g, s_ol, s_or, r_or, s_on, s_dq,
):
    me = lax.axis_index("ctx")
    p = lax.rem(me, 2)
    j = lax.rem(me // 2, RING)
    r = me // (2 * RING)

    def dev(row, col, core):
        return row * (2 * RING) + col * 2 + core

    j_up, j_dn = lax.rem(j + 1, RING), lax.rem(j + RING - 1, RING)
    r_nx, r_pv = lax.rem(r + 1, rows), lax.rem(r + rows - 1, rows)
    sib = dev(r, j, 1 - p)
    up, dn, nxt, prev = dev(r, j_up, p), dev(r, j_dn, p), dev(r_nx, j, p), dev(r_pv, j, p)

    set_up = jnp.where(j < RING - 1, HERE, BEFORE)
    set_down = jnp.where(j > 0, BEFORE, HERE)
    set_far = jnp.where(j < RING // 2, HERE, BEFORE)

    def remote(src, dst, ss, rs, to):
        return pltpu.make_async_remote_copy(
            src_ref=src, dst_ref=dst, send_sem=ss, recv_sem=rs,
            device_id=(to,), device_id_type=pl.DeviceIdType.MESH,
        )

    def cols(plane, g):
        return pl.ds(pl.multiple_of((plane * nh + g) * HD, HD), HD)

    def swap_place(n, g, core):
        return qd.at[OWN, g, core, n] if n < 2 else kv.at[g, HERE, core, n - 2]

    def swap_local(n, g):
        return pltpu.make_async_copy(
            (q, do, kc, vc)[n].at[:, cols(p, g)], swap_place(n, g, p), s_loc.at[n, g]
        )

    def swap_send(n, g):
        return remote(
            (q, do, kc, vc)[n].at[:, cols(1 - p, g)], swap_place(n, g, p), s_d2d.at[n, g],
            r_d2d.at[n, g], sib,
        )

    def swap_recv(n, g):
        return remote(
            (q, do, kc, vc)[n].at[:, cols(1 - p, g)], swap_place(n, g, 1 - p), s_d2d.at[n, g],
            r_d2d.at[n, g], sib,
        )

    queries, clean = (0, 1), (2, 3)

    def swap_start(which, g):
        for n in which:
            swap_send(n, g).start()
        for n in which:
            swap_local(n, g).start()

    def swap_wait(which, g):
        for n in which:
            swap_local(n, g).wait()
            swap_recv(n, g).wait_recv()

    def keys_on(h, g):
        return remote(kv.at[g, HERE, h], kv.at[g, BEFORE, h], s_kb.at[h, g], r_kb.at[h, g], nxt)

    def first_query(d, plane, n):
        return remote(
            (q, do)[n].at[:, cols(plane, 0)], qd.at[(UP, DOWN)[d], 0, p, n],
            s_q0.at[d, plane, n], r_q0.at[d, p, n], dev(r, (j_dn, j_up)[d], plane),
        )

    def first_query_recv(d, core, n):
        return remote(
            (q, do)[n].at[:, cols(core, 0)], qd.at[(UP, DOWN)[d], 0, core, n],
            s_q0.at[d, core, n], r_q0.at[d, core, n], up,
        )

    def first_keys(plane, n):
        return remote(
            (kc, vc)[n].at[:, cols(plane, 0)], kv.at[0, BEFORE, p, n],
            s_k0.at[plane, n], r_k0.at[p, n], dev(r_nx, j, plane),
        )

    def first_keys_recv(core, n):
        return remote(
            (kc, vc)[n].at[:, cols(core, 0)], kv.at[0, BEFORE, core, n],
            s_k0.at[core, n], r_k0.at[core, n], nxt,
        )

    def keys_wait(h, g):
        @pl.when(g == 0)
        def _():
            for n in range(2):
                first_keys_recv(h, n).wait_recv()

        @pl.when(g > 0)
        def _():
            keys_on(h, g).wait_recv()

    class Load:
        def __init__(self, ref, i, stats):
            self.i = i
            self.at = (lambda s: ref.at[s]) if stats else (lambda s: ref.at[s, i])
            self.blk = (lambda s, b: ref.at[s, b]) if stats else (lambda s, b: ref.at[s, i, b])

        def down(self):
            return remote(self.at(OWN), self.at(UP), s_dn.at[self.i], r_dn.at[self.i], dn)

        def up(self):
            return remote(self.at(OWN), self.at(DOWN), s_up.at[self.i], r_up.at[self.i], up)

        def relay_down(self):
            return remote(self.blk(UP, 0), self.blk(FAR, 0), s_rd.at[self.i], r_far.at[0, self.i], dn)

        def relay_up(self):
            return remote(self.blk(DOWN, 1), self.blk(FAR, 1), s_ru.at[self.i], r_far.at[1, self.i], up)

        def send_own(self):
            self.down().start()
            self.up().start()

        def relay(self):
            self.down().wait_recv()
            self.relay_down().start()
            self.up().wait_recv()
            self.relay_up().start()

        def far_wait(self):
            self.relay_down().wait_recv()
            self.relay_up().wait_recv()

        def done_own(self):
            self.down().wait_send()
            self.up().wait_send()

        def done(self):
            self.relay_down().wait_send()
            self.relay_up().wait_send()

    def load(g):
        return Load(qd, g, False)

    stats = Load(st, nh, True)

    def far_copy(d, g):
        return remote(fs.at[d, g], fr.at[d, g], s_f.at[d, g], r_f.at[d, g], (up, dn)[d])

    def near_copy(d, b, g):
        return remote(
            ns.at[d, g, b], nr.at[d, g, p], s_n.at[d, b, g], r_n.at[d, p, g],
            dev(r, (j_up, j_dn)[d], b),
        )

    def near_recv(d, plane, g):
        return remote(
            ns.at[d, g, plane], nr.at[d, g, plane], s_n.at[d, plane, g], r_n.at[d, plane, g], up
        )

    def back_copy(h, g):
        return remote(db.at[g, h], dr.at[g, h], s_b.at[h, g], r_b.at[h, g], prev)

    def own_copy(g):
        return remote(gs.at[g], gr.at[g], s_g.at[g], r_g.at[g], sib)

    def out_local(n, g):
        return pltpu.make_async_copy(
            dr.at[g, p, n], (dkc, dvc)[n].at[:, cols(p, g)], s_ol.at[n, g]
        )

    def out_remote(n, g):
        return remote(
            dr.at[g, 1 - p, n], (dkc, dvc)[n].at[:, cols(p, g)], s_or.at[n, g], r_or.at[n, g], sib
        )

    def out_recv(n, g):
        return remote(
            dr.at[g, p, n], (dkc, dvc)[n].at[:, cols(1 - p, g)], s_or.at[n, g], r_or.at[n, g], sib
        )

    def mine_copy(n):
        return pltpu.make_async_copy((q, do, kn, vn)[n], mine.at[n], s_mine.at[n])

    def noised_out(n, plane, g):
        c = cols(plane, g)
        return pltpu.make_async_copy(
            mine.at[2 + n, :, c], (dkn, dvn)[n].at[:, c], s_on.at[n, plane, g]
        )

    def dq_out(plane, g):
        return pltpu.make_async_copy(
            dqs.at[:, cols(plane, g)], dq.at[:, cols(plane, g)], s_dq.at[plane, g]
        )

    def grads(query, grad_out, keys, values, bias, deltas):
        s = dot_nt(keys, query)
        dp = dot_nt(values, grad_out)
        x = jnp.concatenate(
            [s[n * BLK : (n + 1) * BLK] * (SCALE * LOG2E) - row for n, row in enumerate(bias)], axis=0
        )
        prob = jnp.exp2(x)
        ds = (prob * (dp - deltas)).astype(BF16)
        return dot_tn(keys, ds), dot_nn(ds, query), dot_nn(prob.astype(BF16), grad_out)

    first_here = (me // 2) * 4
    first_before = (r_pv * RING + j) * 4

    def item(slot, b, g, h, keys_set, first=False):
        first_id = jnp.where(keys_set == HERE, first_here, first_before) + 2 * h
        place = jnp.where(keys_set == HERE, lax.rem(2 * g + h, 4), 4)
        ids = st[slot, b, 16:24, :]
        log_sums = st[slot, b, pl.ds(g, 1), :]
        bias = []
        for c in range(2):
            miss = jnp.min(jnp.abs(ids - (first_id + c).astype(F32)), axis=0, keepdims=True)
            bias.append(log_sums + jnp.minimum(miss, 1.0) * FAR_OFF)
        d_q, d_k, d_v = grads(
            qd[slot, g, b, 0], qd[slot, g, b, 1], kv[g, keys_set, h, 0], kv[g, keys_set, h, 1],
            bias, st[slot, b, pl.ds(8 + g, 1), :],
        )
        if first:
            acc[place, 0], acc[place, 1] = d_k, d_v
        else:
            acc[place, 0] += d_k
            acc[place, 1] += d_v
        return d_q

    def own_pairs(g):
        for plane in range(2):
            h, c = plane * nh + g, cols(plane, g)
            d_q, d_k, d_v = grads(
                mine[0, :, c], mine[1, :, c], mine[2, :, c], mine[3, :, c],
                [lv[pl.ds(h, 1), :] * LOG2E], dv[pl.ds(h, 1), :],
            )
            oq[h] = d_q
            mine[2, :, c] = (d_k * SCALE).astype(BF16)
            mine[3, :, c] = d_v.astype(BF16)
        for n in range(2):
            for plane in range(2):
                noised_out(n, plane, g).start()

    def send_keys_grads(h, g):
        for n in range(2):
            db[g, h, n] = acc[4, n].astype(BF16)
        back_copy(h, g).start()

    def first_half(g):
        keys_wait(0, g)

        @pl.when(g + 1 < nh)
        def _():
            swap_wait(clean, g + 1)
            keys_on(0, g + 1).start()

        part[OWN, 0] = item(OWN, 0, g, 0, BEFORE, first=True)
        part[OWN, 1] = item(OWN, 1, g, 0, HERE, first=True)
        for b in range(2):
            part[DOWN, b] = item(DOWN, b, g, 0, set_down)
        for b in range(2):
            part[UP, b] = item(UP, b, g, 0, set_up)

        @pl.when(g >= 2)
        def _():
            send_near(g - 2)

        @pl.when(g == 0)
        def _():
            stats.far_wait()

        load(g).far_wait()
        for b in range(2):
            part[FAR, b] = item(FAR, b, g, 0, set_far)
        send_keys_grads(0, g)

    def second_half(g):
        keys_wait(1, g)

        @pl.when(g + 1 < nh)
        def _():
            keys_on(1, g + 1).start()

        for n in range(2):
            acc[lax.rem(2 * g + 1, 4), n] = jnp.zeros((CLEAN, HD), F32)
        own_0 = part[OWN, 0] + item(OWN, 0, g, 1, BEFORE, first=True)
        for b in range(2):
            fs[b, g] = (part[FAR, b] + item(FAR, b, g, 1, set_far)).astype(BF16)
        for d in range(2):
            far_copy(d, g).start()

        @pl.when(g + 2 < nh)
        def _():
            swap_wait(queries, g + 2)
            load(g + 2).send_own()

        own_1 = part[OWN, 1] + item(OWN, 1, g, 1, BEFORE)
        oq[p * nh + g] += jnp.where(p == 0, own_0, own_1)
        gs[g] = jnp.where(p == 0, own_1, own_0).astype(BF16)
        own_copy(g).start()
        ns[1, g, 0] = (part[DOWN, 0] + item(DOWN, 0, g, 1, set_down)).astype(BF16)
        near_copy(1, 0, g).start()
        near_p[lax.rem(g, 2), 1] = part[DOWN, 1] + item(DOWN, 1, g, 1, set_down)
        ns[0, g, 1] = (part[UP, 1] + item(UP, 1, g, 1, set_up)).astype(BF16)
        near_copy(0, 1, g).start()
        near_p[lax.rem(g, 2), 0] = part[UP, 0] + item(UP, 0, g, 1, set_up)
        send_keys_grads(1, g)

    def send_near(g):
        for d in range(2):
            far_copy(d, g).wait_recv()
            ns[d, g, d] = (near_p[lax.rem(g, 2), d] + fr[d, g].astype(F32)).astype(BF16)
            near_copy(d, d, g).start()

    def finish_clean(h, g):
        back_copy(h, g).wait_recv()
        for n in range(2):
            total = acc[lax.rem(2 * g + h, 4), n] + dr[g, h, n].astype(F32)
            dr[g, h, n] = (total * (SCALE if n == 0 else 1.0)).astype(BF16)

        @pl.when(p == h)
        def _():
            for n in range(2):
                out_local(n, g).start()

        @pl.when(p != h)
        def _():
            for n in range(2):
                out_remote(n, g).start()

    def finish(g):
        own_copy(g).wait_recv()
        oq[(1 - p) * nh + g] += gr[g].astype(F32)
        for plane in range(2):
            for d in range(2):
                near_recv(d, plane, g).wait_recv()
            total = oq[plane * nh + g] + nr[0, g, plane].astype(F32) + nr[1, g, plane].astype(F32)
            dqs[:, cols(plane, g)] = (total * SCALE).T.astype(BF16)
            dq_out(plane, g).start()

    def drain(g):
        for n in range(4):
            swap_send(n, g).wait_send()
        load(g).done()

        @pl.when(g > 0)
        def _():
            load(g).done_own()
            for h in range(2):
                keys_on(h, g).wait_send()

        @pl.when(g == 0)
        def _():
            for plane in range(2):
                for n in range(2):
                    first_keys(plane, n).wait_send()
                    for d in range(2):
                        first_query(d, plane, n).wait_send()

        own_copy(g).wait_send()
        for n in range(2):
            for m in range(2):
                near_copy(n, m, g).wait_send()
                noised_out(n, m, g).wait()
            far_copy(n, g).wait_send()
            back_copy(n, g).wait_send()
            dq_out(n, g).wait()
            out_local(n, g).wait()
            out_remote(n, g).wait_send()
            out_recv(n, g).wait_recv()

    barrier = pltpu.get_barrier_semaphore()
    greeted = [sib, nxt, prev, dev(r_nx, j, 1 - p), dev(r_pv, j, 1 - p)] + [dev(r, col, core) for col in (j_up, j_dn) for core in range(2)]
    for other in greeted:
        pl.semaphore_signal(
            barrier, inc=1, device_id=(other,), device_id_type=pl.DeviceIdType.MESH
        )
    in_lse = pltpu.make_async_copy(lse, lv, s_in.at[0])
    in_delta = pltpu.make_async_copy(delta, dv, s_in.at[1])
    in_listed = pltpu.make_async_copy(listed, lm, s_in.at[2])
    in_lse.start()
    in_delta.start()
    in_listed.start()

    def stats_swap(blk):
        return remote(ms.at[1 - p], st.at[OWN, blk], s_sd.at[0], r_sd.at[0], sib)

    pl.semaphore_wait(barrier, len(greeted))
    for n in range(2):
        for plane in range(2):
            for d in range(2):
                first_query(d, plane, n).start()
    for n in range(2):
        for plane in range(2):
            first_keys(plane, n).start()
    swap_start(queries, 0)
    swap_start(clean, 0)
    in_lse.wait()
    in_delta.wait()
    in_listed.wait()
    for plane in range(2):
        ms[plane, 0:nh] = lv[plane * nh : (plane + 1) * nh] * LOG2E
        ms[plane, 8 : 8 + nh] = dv[plane * nh : (plane + 1) * nh]
        for n in range(8):
            ms[plane, 16 + n : 17 + n] = jnp.full((1, BLK), lm[0, n].astype(F32))
    st[OWN, p] = ms[p]
    stats_swap(p).start()
    stats_swap(1 - p).wait_recv()
    stats.send_own()
    for g in range(1, min(3, nh)):
        swap_start(queries, g)
    for g in range(1, min(2, nh)):
        swap_start(clean, g)
    for n in range(4):
        mine_copy(n).start()
    for d in range(2):
        for n in range(2):
            for core in range(2):
                first_query_recv(d, core, n).wait_recv()
    load(0).relay_down().start()
    load(0).relay_up().start()
    stats.relay()
    swap_wait(queries, 0)
    swap_wait(clean, 0)
    if nh > 1:
        swap_wait(queries, 1)
        load(1).send_own()

    def step(t, _):
        @pl.when(t + 3 < nh)
        def _():
            swap_start(queries, t + 3)

        @pl.when(t + 2 < nh)
        def _():
            swap_start(clean, t + 2)

        first_half(t)

        @pl.when(t == 0)
        def _():
            for n in range(4):
                mine_copy(n).wait()

        own_pairs(t)

        @pl.when(t + 1 < nh)
        def _():
            load(t + 1).relay()

        second_half(t)

        @pl.when(t >= 1)
        def _():
            finish_clean(0, t - 1)
            finish_clean(1, t - 1)

        @pl.when(t >= 3)
        def _():
            finish(t - 3)

        @pl.when(t >= 4)
        def _():
            drain(t - 4)

        return 0

    lax.fori_loop(0, nh, step, 0)
    for g in range(max(nh - 2, 0), nh):
        send_near(g)
    finish_clean(0, nh - 1)
    for g in range(max(nh - 4, 0), nh - 1):
        if g >= nh - 3:
            finish(g)
        drain(g)
    stats_swap(p).wait_send()
    stats.done_own()
    stats.done()
    finish_clean(1, nh - 1)
    finish(nh - 1)
    drain(nh - 1)


def copy_out(*refs):
    sources, results, held, arrive, leave = refs[:5], refs[5:10], refs[10:15], refs[15], refs[16]
    into = [pltpu.make_async_copy(sources[n], held[n], arrive.at[n]) for n in range(5)]
    out = [pltpu.make_async_copy(held[n], results[n], leave.at[n]) for n in range(5)]
    for copy in into:
        copy.start()
    for one, two in zip(into, out, strict=True):
        one.wait()
        two.start()
    for copy in out:
        copy.wait()


def per_device(rows, q_noised, k_noised, v_noised, dout, lse, delta, listed, k_clean, v_clean):
    width = q_noised.shape[1]
    nh = width // HD // 2
    vm, dma = pltpu.VMEM, pltpu.SemaphoreType.DMA
    hbm = pl.BlockSpec(memory_space=pl.ANY)
    tile = (HD, BLK)
    scratch = [
        vm((4, nh, 2, 2, BLK, HD), BF16),
        vm((nh, 2, 2, 2, CLEAN, HD), BF16),
        vm((2 * nh, BLK), F32),
        vm((2 * nh, BLK), F32),
        vm((2, STAT, BLK), F32),
        vm((4, 2, STAT, BLK), F32),
        vm((4, BLK, width), BF16),
        vm((2 * nh, *tile), F32),
        vm((4, 2, *tile), F32),
        vm((2, 2, *tile), F32),
        vm((5, 2, CLEAN, HD), F32),
        vm((nh, 2, 2, CLEAN, HD), BF16),
        vm((nh, 2, 2, CLEAN, HD), BF16),
        vm((2, nh, *tile), BF16),
        vm((2, nh, *tile), BF16),
        vm((2, nh, 2, *tile), BF16),
        vm((2, nh, 2, *tile), BF16),
        vm((nh, *tile), BF16),
        vm((nh, *tile), BF16),
        vm((BLK, width), BF16),
        pltpu.SMEM((1, 8), jnp.int32),
        dma((3,)),
        dma((4,)),
        dma((4, nh)),
        dma((4, nh)),
        dma((4, nh)),
        dma((1,)),
        dma((1,)),
        dma((2, nh)),
        dma((2, nh)),
        dma((2, 2, 2)),
        dma((2, 2, 2)),
        dma((2, 2)),
        dma((2, 2)),
        *[dma((nh + 1,)) for _ in range(6)],
        dma((2, nh + 1)),
        dma((2, nh)),
        dma((2, nh)),
        dma((2, 2, nh)),
        dma((2, 2, nh)),
        dma((2, nh)),
        dma((2, nh)),
        dma((nh,)),
        dma((nh,)),
        dma((2, nh)),
        dma((2, nh)),
        dma((2, nh)),
        dma((2, 2, nh)),
        dma((2, nh)),
    ]
    pairs = 17 * 2 * nh
    outs = pl.pallas_call(
        functools.partial(kernel, rows, nh),
        out_shape=[jax.ShapeDtypeStruct((BLK, width), BF16)] * 3
        + [jax.ShapeDtypeStruct((CLEAN, width), BF16)] * 2,
        in_specs=[hbm] * 9,
        out_specs=[hbm] * 5,
        scratch_shapes=scratch,
        compiler_params=pltpu.CompilerParams(
            collective_id=0, has_side_effects=True, vmem_limit_bytes=60 * 2**20
        ),
        cost_estimate=pl.CostEstimate(
            flops=pairs * 10 * BLK * BLK * HD,
            bytes_accessed=15 * 2**20,
            transcendentals=pairs * BLK * BLK,
        ),
        name="block_attention_backward",
    )(q_noised, dout, k_noised, v_noised, k_clean, v_clean, lse, delta, listed)
    return pl.pallas_call(
        copy_out,
        out_shape=[jax.ShapeDtypeStruct(out.shape, out.dtype) for out in outs],
        in_specs=[hbm] * 5,
        out_specs=[hbm] * 5,
        scratch_shapes=[vm(out.shape, out.dtype) for out in outs] + [dma((5,)), dma((5,))],
        name="copy_out",
    )(*outs)


def solution(mesh):
    rows = mesh.shape["ctx"] // (2 * RING)
    split = P("ctx", None)
    return jax.shard_map(
        functools.partial(per_device, rows),
        mesh=mesh,
        in_specs=(split,) * 4 + (P(None, "ctx"),) * 2 + (split,) * 3,
        out_specs=(split,) * 5,
        check_vma=False,
    )
```

```python
import functools

import jax
import jax.numpy as jnp
from jax import lax
from jax.experimental import pallas as pl
from jax.experimental.pallas import tpu as pltpu
from jax.sharding import PartitionSpec as P

F32 = jnp.float32
BF16 = jnp.bfloat16
HD = 128
BLK = 256
CLEAN = 512
RING = 4
SCALE = HD**-0.5
LOG2E = 1.4426950408889634
FAR_OFF = 1e30
STAT = 24

OWN, UP, DOWN, FAR = range(4)
HERE, BEFORE = range(2)


def dot_nt(a, b):
    return lax.dot_general(a, b, (((1,), (1,)), ((), ())), preferred_element_type=F32)


def dot_nn(a, b):
    return lax.dot_general(a, b, (((1,), (0,)), ((), ())), preferred_element_type=F32)


def dot_tn(a, b):
    return lax.dot_general(a, b, (((0,), (0,)), ((), ())), preferred_element_type=F32)


def kernel(
    rows, nh,
    q, do, kn, vn, kc, vc, lse, delta, listed,
    dq, dkn, dvn, dkc, dvc,
    qd, kv, lv, dv, ms, st, mine, oq, part, near_p, acc, db, dr, fs, fr, ns, nr, gs, gr, dqs,
    lm, s_in, s_mine, s_loc, s_d2d, r_d2d, s_sd, r_sd, s_kb, r_kb,
    s_q0, r_q0, s_k0, r_k0,
    s_dn, r_dn, s_up, r_up, s_rd, s_ru, r_far,
    s_f, r_f, s_n, r_n, s_b, r_b, s_g, r_g, s_ol, s_or, r_or, s_on, s_dq,
):
    me = lax.axis_index("ctx")
    p = lax.rem(me, 2)
    j = lax.rem(me // 2, RING)
    r = me // (2 * RING)

    def dev(row, col, core):
        return row * (2 * RING) + col * 2 + core

    j_up, j_dn = lax.rem(j + 1, RING), lax.rem(j + RING - 1, RING)
    r_nx, r_pv = lax.rem(r + 1, rows), lax.rem(r + rows - 1, rows)
    sib = dev(r, j, 1 - p)
    up, dn, nxt, prev = dev(r, j_up, p), dev(r, j_dn, p), dev(r_nx, j, p), dev(r_pv, j, p)

    set_up = jnp.where(j < RING - 1, HERE, BEFORE)
    set_down = jnp.where(j > 0, BEFORE, HERE)
    set_far = jnp.where(j < RING // 2, HERE, BEFORE)

    def remote(src, dst, ss, rs, to):
        return pltpu.make_async_remote_copy(
            src_ref=src, dst_ref=dst, send_sem=ss, recv_sem=rs,
            device_id=(to,), device_id_type=pl.DeviceIdType.MESH,
        )

    def cols(plane, g):
        return pl.ds(pl.multiple_of((plane * nh + g) * HD, HD), HD)

    def swap_place(n, g, core):
        return qd.at[OWN, g, core, n] if n < 2 else kv.at[g, HERE, core, n - 2]

    def swap_local(n, g):
        return pltpu.make_async_copy(
            (q, do, kc, vc)[n].at[:, cols(p, g)], swap_place(n, g, p), s_loc.at[n, g]
        )

    def swap_send(n, g):
        return remote(
            (q, do, kc, vc)[n].at[:, cols(1 - p, g)], swap_place(n, g, p), s_d2d.at[n, g],
            r_d2d.at[n, g], sib,
        )

    def swap_recv(n, g):
        return remote(
            (q, do, kc, vc)[n].at[:, cols(1 - p, g)], swap_place(n, g, 1 - p), s_d2d.at[n, g],
            r_d2d.at[n, g], sib,
        )

    queries, clean = (0, 1), (2, 3)

    def swap_start(which, g):
        for n in which:
            swap_send(n, g).start()
        for n in which:
            swap_local(n, g).start()

    def swap_wait(which, g):
        for n in which:
            swap_local(n, g).wait()
            swap_recv(n, g).wait_recv()

    def keys_on(h, g):
        return remote(kv.at[g, HERE, h], kv.at[g, BEFORE, h], s_kb.at[h, g], r_kb.at[h, g], nxt)

    def first_query(d, plane, n):
        return remote(
            (q, do)[n].at[:, cols(plane, 0)], qd.at[(UP, DOWN)[d], 0, p, n],
            s_q0.at[d, plane, n], r_q0.at[d, p, n], dev(r, (j_dn, j_up)[d], plane),
        )

    def first_query_recv(d, core, n):
        return remote(
            (q, do)[n].at[:, cols(core, 0)], qd.at[(UP, DOWN)[d], 0, core, n],
            s_q0.at[d, core, n], r_q0.at[d, core, n], up,
        )

    def first_keys(plane, n):
        return remote(
            (kc, vc)[n].at[:, cols(plane, 0)], kv.at[0, BEFORE, p, n],
            s_k0.at[plane, n], r_k0.at[p, n], dev(r_nx, j, plane),
        )

    def first_keys_recv(core, n):
        return remote(
            (kc, vc)[n].at[:, cols(core, 0)], kv.at[0, BEFORE, core, n],
            s_k0.at[core, n], r_k0.at[core, n], nxt,
        )

    def keys_wait(h, g):
        @pl.when(g == 0)
        def _():
            for n in range(2):
                first_keys_recv(h, n).wait_recv()

        @pl.when(g > 0)
        def _():
            keys_on(h, g).wait_recv()

    class Load:
        def __init__(self, ref, i, stats):
            self.i = i
            self.at = (lambda s: ref.at[s]) if stats else (lambda s: ref.at[s, i])
            self.blk = (lambda s, b: ref.at[s, b]) if stats else (lambda s, b: ref.at[s, i, b])

        def down(self):
            return remote(self.at(OWN), self.at(UP), s_dn.at[self.i], r_dn.at[self.i], dn)

        def up(self):
            return remote(self.at(OWN), self.at(DOWN), s_up.at[self.i], r_up.at[self.i], up)

        def relay_down(self):
            return remote(self.blk(UP, 0), self.blk(FAR, 0), s_rd.at[self.i], r_far.at[0, self.i], dn)

        def relay_up(self):
            return remote(self.blk(DOWN, 1), self.blk(FAR, 1), s_ru.at[self.i], r_far.at[1, self.i], up)

        def send_own(self):
            self.down().start()
            self.up().start()

        def relay(self):
            self.down().wait_recv()
            self.relay_down().start()
            self.up().wait_recv()
            self.relay_up().start()

        def far_wait(self):
            self.relay_down().wait_recv()
            self.relay_up().wait_recv()

        def done_own(self):
            self.down().wait_send()
            self.up().wait_send()

        def done(self):
            self.relay_down().wait_send()
            self.relay_up().wait_send()

    def load(g):
        return Load(qd, g, False)

    stats = Load(st, nh, True)

    def far_copy(d, g):
        return remote(fs.at[d, g], fr.at[d, g], s_f.at[d, g], r_f.at[d, g], (up, dn)[d])

    def near_copy(d, b, g):
        return remote(
            ns.at[d, g, b], nr.at[d, g, p], s_n.at[d, b, g], r_n.at[d, p, g],
            dev(r, (j_up, j_dn)[d], b),
        )

    def near_recv(d, plane, g):
        return remote(
            ns.at[d, g, plane], nr.at[d, g, plane], s_n.at[d, plane, g], r_n.at[d, plane, g], up
        )

    def back_copy(h, g):
        return remote(db.at[g, h], dr.at[g, h], s_b.at[h, g], r_b.at[h, g], prev)

    def own_copy(g):
        return remote(gs.at[g], gr.at[g], s_g.at[g], r_g.at[g], sib)

    def out_local(n, g):
        return pltpu.make_async_copy(
            dr.at[g, p, n], (dkc, dvc)[n].at[:, cols(p, g)], s_ol.at[n, g]
        )

    def out_remote(n, g):
        return remote(
            dr.at[g, 1 - p, n], (dkc, dvc)[n].at[:, cols(p, g)], s_or.at[n, g], r_or.at[n, g], sib
        )

    def out_recv(n, g):
        return remote(
            dr.at[g, p, n], (dkc, dvc)[n].at[:, cols(1 - p, g)], s_or.at[n, g], r_or.at[n, g], sib
        )

    def mine_copy(n):
        return pltpu.make_async_copy((q, do, kn, vn)[n], mine.at[n], s_mine.at[n])

    def noised_out(n, plane, g):
        c = cols(plane, g)
        return pltpu.make_async_copy(
            mine.at[2 + n, :, c], (dkn, dvn)[n].at[:, c], s_on.at[n, plane, g]
        )

    def dq_out(plane, g):
        return pltpu.make_async_copy(
            dqs.at[:, cols(plane, g)], dq.at[:, cols(plane, g)], s_dq.at[plane, g]
        )

    def grads(query, grad_out, keys, values, bias, deltas):
        s = dot_nt(keys, query)
        dp = dot_nt(values, grad_out)
        x = jnp.concatenate(
            [s[n * BLK : (n + 1) * BLK] * (SCALE * LOG2E) - row for n, row in enumerate(bias)], axis=0
        )
        prob = jnp.exp2(x)
        ds = (prob * (dp - deltas)).astype(BF16)
        return dot_tn(keys, ds), dot_nn(ds, query), dot_nn(prob.astype(BF16), grad_out)

    first_here = (me // 2) * 4
    first_before = (r_pv * RING + j) * 4

    def item(slot, b, g, h, keys_set, first=False):
        first_id = jnp.where(keys_set == HERE, first_here, first_before) + 2 * h
        place = jnp.where(keys_set == HERE, lax.rem(2 * g + h, 4), 4)
        ids = st[slot, b, 16:24, :]
        log_sums = st[slot, b, pl.ds(g, 1), :]
        bias = []
        for c in range(2):
            miss = jnp.min(jnp.abs(ids - (first_id + c).astype(F32)), axis=0, keepdims=True)
            bias.append(log_sums + jnp.minimum(miss, 1.0) * FAR_OFF)
        d_q, d_k, d_v = grads(
            qd[slot, g, b, 0], qd[slot, g, b, 1], kv[g, keys_set, h, 0], kv[g, keys_set, h, 1],
            bias, st[slot, b, pl.ds(8 + g, 1), :],
        )
        if first:
            acc[place, 0], acc[place, 1] = d_k, d_v
        else:
            acc[place, 0] += d_k
            acc[place, 1] += d_v
        return d_q

    def own_pairs(g):
        for plane in range(2):
            h, c = plane * nh + g, cols(plane, g)
            d_q, d_k, d_v = grads(
                mine[0, :, c], mine[1, :, c], mine[2, :, c], mine[3, :, c],
                [lv[pl.ds(h, 1), :] * LOG2E], dv[pl.ds(h, 1), :],
            )
            oq[h] = d_q
            mine[2, :, c] = (d_k * SCALE).astype(BF16)
            mine[3, :, c] = d_v.astype(BF16)
        for n in range(2):
            for plane in range(2):
                noised_out(n, plane, g).start()

    def send_keys_grads(h, g):
        for n in range(2):
            db[g, h, n] = acc[4, n].astype(BF16)
        back_copy(h, g).start()

    def first_half(g):
        keys_wait(0, g)

        @pl.when(g + 1 < nh)
        def _():
            swap_wait(clean, g + 1)
            keys_on(0, g + 1).start()

        part[OWN, 0] = item(OWN, 0, g, 0, BEFORE, first=True)
        part[OWN, 1] = item(OWN, 1, g, 0, HERE, first=True)
        for b in range(2):
            part[DOWN, b] = item(DOWN, b, g, 0, set_down)
        for b in range(2):
            part[UP, b] = item(UP, b, g, 0, set_up)

        @pl.when(g >= 2)
        def _():
            send_near(g - 2)

        @pl.when(g == 0)
        def _():
            stats.far_wait()

        load(g).far_wait()
        for b in range(2):
            part[FAR, b] = item(FAR, b, g, 0, set_far)
        send_keys_grads(0, g)

    def second_half(g):
        keys_wait(1, g)

        @pl.when(g + 1 < nh)
        def _():
            keys_on(1, g + 1).start()

        for n in range(2):
            acc[lax.rem(2 * g + 1, 4), n] = jnp.zeros((CLEAN, HD), F32)
        own_0 = part[OWN, 0] + item(OWN, 0, g, 1, BEFORE, first=True)
        for b in range(2):
            fs[b, g] = (part[FAR, b] + item(FAR, b, g, 1, set_far)).astype(BF16)
        for d in range(2):
            far_copy(d, g).start()

        @pl.when(g + 2 < nh)
        def _():
            swap_wait(queries, g + 2)
            load(g + 2).send_own()

        own_1 = part[OWN, 1] + item(OWN, 1, g, 1, BEFORE)
        oq[p * nh + g] += jnp.where(p == 0, own_0, own_1)
        gs[g] = jnp.where(p == 0, own_1, own_0).astype(BF16)
        own_copy(g).start()
        ns[1, g, 0] = (part[DOWN, 0] + item(DOWN, 0, g, 1, set_down)).astype(BF16)
        near_copy(1, 0, g).start()
        near_p[lax.rem(g, 2), 1] = part[DOWN, 1] + item(DOWN, 1, g, 1, set_down)
        ns[0, g, 1] = (part[UP, 1] + item(UP, 1, g, 1, set_up)).astype(BF16)
        near_copy(0, 1, g).start()
        near_p[lax.rem(g, 2), 0] = part[UP, 0] + item(UP, 0, g, 1, set_up)
        send_keys_grads(1, g)

    def send_near(g):
        for d in range(2):
            far_copy(d, g).wait_recv()
            ns[d, g, d] = (near_p[lax.rem(g, 2), d] + fr[d, g].astype(F32)).astype(BF16)
            near_copy(d, d, g).start()

    def finish_clean(h, g):
        back_copy(h, g).wait_recv()
        for n in range(2):
            total = acc[lax.rem(2 * g + h, 4), n] + dr[g, h, n].astype(F32)
            dr[g, h, n] = (total * (SCALE if n == 0 else 1.0)).astype(BF16)

        @pl.when(p == h)
        def _():
            for n in range(2):
                out_local(n, g).start()

        @pl.when(p != h)
        def _():
            for n in range(2):
                out_remote(n, g).start()

    def finish(g):
        own_copy(g).wait_recv()
        oq[(1 - p) * nh + g] += gr[g].astype(F32)
        for plane in range(2):
            for d in range(2):
                near_recv(d, plane, g).wait_recv()
            total = oq[plane * nh + g] + nr[0, g, plane].astype(F32) + nr[1, g, plane].astype(F32)
            dqs[:, cols(plane, g)] = (total * SCALE).T.astype(BF16)
            dq_out(plane, g).start()

    def drain(g):
        for n in range(4):
            swap_send(n, g).wait_send()
        load(g).done()

        @pl.when(g > 0)
        def _():
            load(g).done_own()
            for h in range(2):
                keys_on(h, g).wait_send()

        @pl.when(g == 0)
        def _():
            for plane in range(2):
                for n in range(2):
                    first_keys(plane, n).wait_send()
                    for d in range(2):
                        first_query(d, plane, n).wait_send()

        own_copy(g).wait_send()
        for n in range(2):
            for m in range(2):
                near_copy(n, m, g).wait_send()
                noised_out(n, m, g).wait()
            far_copy(n, g).wait_send()
            back_copy(n, g).wait_send()
            dq_out(n, g).wait()
            out_local(n, g).wait()
            out_remote(n, g).wait_send()
            out_recv(n, g).wait_recv()

    barrier = pltpu.get_barrier_semaphore()
    greeted = [sib, nxt, prev, dev(r_nx, j, 1 - p), dev(r_pv, j, 1 - p)] + [dev(r, col, core) for col in (j_up, j_dn) for core in range(2)]
    for other in greeted:
        pl.semaphore_signal(
            barrier, inc=1, device_id=(other,), device_id_type=pl.DeviceIdType.MESH
        )
    in_lse = pltpu.make_async_copy(lse, lv, s_in.at[0])
    in_delta = pltpu.make_async_copy(delta, dv, s_in.at[1])
    in_listed = pltpu.make_async_copy(listed, lm, s_in.at[2])
    in_lse.start()
    in_delta.start()
    in_listed.start()

    def stats_swap(blk):
        return remote(ms.at[1 - p], st.at[OWN, blk], s_sd.at[0], r_sd.at[0], sib)

    pl.semaphore_wait(barrier, len(greeted))
    for n in range(2):
        for plane in range(2):
            for d in range(2):
                first_query(d, plane, n).start()
    for n in range(2):
        for plane in range(2):
            first_keys(plane, n).start()
    swap_start(queries, 0)
    swap_start(clean, 0)
    in_lse.wait()
    in_delta.wait()
    in_listed.wait()
    for plane in range(2):
        ms[plane, 0:nh] = lv[plane * nh : (plane + 1) * nh] * LOG2E
        ms[plane, 8 : 8 + nh] = dv[plane * nh : (plane + 1) * nh]
        for n in range(8):
            ms[plane, 16 + n : 17 + n] = jnp.full((1, BLK), lm[0, n].astype(F32))
    st[OWN, p] = ms[p]
    stats_swap(p).start()
    stats_swap(1 - p).wait_recv()
    stats.send_own()
    for g in range(1, min(3, nh)):
        swap_start(queries, g)
    for g in range(1, min(2, nh)):
        swap_start(clean, g)
    for n in range(4):
        mine_copy(n).start()
    for n in range(4):
        mine_copy(n).wait()
    own_pairs(0)
    for d in range(2):
        for n in range(2):
            for core in range(2):
                first_query_recv(d, core, n).wait_recv()
    load(0).relay_down().start()
    load(0).relay_up().start()
    stats.relay()
    swap_wait(queries, 0)
    swap_wait(clean, 0)
    if nh > 1:
        swap_wait(queries, 1)
        load(1).send_own()

    def step(t, _):
        @pl.when(t + 3 < nh)
        def _():
            swap_start(queries, t + 3)

        @pl.when(t + 2 < nh)
        def _():
            swap_start(clean, t + 2)

        first_half(t)

        @pl.when(t + 1 < nh)
        def _():
            own_pairs(t + 1)

        @pl.when(t + 1 < nh)
        def _():
            load(t + 1).relay()

        second_half(t)

        @pl.when(t >= 1)
        def _():
            finish_clean(0, t - 1)
            finish_clean(1, t - 1)

        @pl.when(t >= 3)
        def _():
            finish(t - 3)

        @pl.when(t >= 4)
        def _():
            drain(t - 4)

        return 0

    lax.fori_loop(0, nh, step, 0)
    for g in range(max(nh - 2, 0), nh):
        send_near(g)
    finish_clean(0, nh - 1)
    for g in range(max(nh - 4, 0), nh - 1):
        if g >= nh - 3:
            finish(g)
        drain(g)
    stats_swap(p).wait_send()
    stats.done_own()
    stats.done()
    finish_clean(1, nh - 1)
    finish(nh - 1)
    drain(nh - 1)


def copy_out(*refs):
    sources, results, held, arrive, leave = refs[:5], refs[5:10], refs[10:15], refs[15], refs[16]
    into = [pltpu.make_async_copy(sources[n], held[n], arrive.at[n]) for n in range(5)]
    out = [pltpu.make_async_copy(held[n], results[n], leave.at[n]) for n in range(5)]
    for copy in into:
        copy.start()
    for one, two in zip(into, out, strict=True):
        one.wait()
        two.start()
    for copy in out:
        copy.wait()


def per_device(rows, q_noised, k_noised, v_noised, dout, lse, delta, listed, k_clean, v_clean):
    width = q_noised.shape[1]
    nh = width // HD // 2
    vm, dma = pltpu.VMEM, pltpu.SemaphoreType.DMA
    hbm = pl.BlockSpec(memory_space=pl.ANY)
    tile = (HD, BLK)
    scratch = [
        vm((4, nh, 2, 2, BLK, HD), BF16),
        vm((nh, 2, 2, 2, CLEAN, HD), BF16),
        vm((2 * nh, BLK), F32),
        vm((2 * nh, BLK), F32),
        vm((2, STAT, BLK), F32),
        vm((4, 2, STAT, BLK), F32),
        vm((4, BLK, width), BF16),
        vm((2 * nh, *tile), F32),
        vm((4, 2, *tile), F32),
        vm((2, 2, *tile), F32),
        vm((5, 2, CLEAN, HD), F32),
        vm((nh, 2, 2, CLEAN, HD), BF16),
        vm((nh, 2, 2, CLEAN, HD), BF16),
        vm((2, nh, *tile), BF16),
        vm((2, nh, *tile), BF16),
        vm((2, nh, 2, *tile), BF16),
        vm((2, nh, 2, *tile), BF16),
        vm((nh, *tile), BF16),
        vm((nh, *tile), BF16),
        vm((BLK, width), BF16),
        pltpu.SMEM((1, 8), jnp.int32),
        dma((3,)),
        dma((4,)),
        dma((4, nh)),
        dma((4, nh)),
        dma((4, nh)),
        dma((1,)),
        dma((1,)),
        dma((2, nh)),
        dma((2, nh)),
        dma((2, 2, 2)),
        dma((2, 2, 2)),
        dma((2, 2)),
        dma((2, 2)),
        *[dma((nh + 1,)) for _ in range(6)],
        dma((2, nh + 1)),
        dma((2, nh)),
        dma((2, nh)),
        dma((2, 2, nh)),
        dma((2, 2, nh)),
        dma((2, nh)),
        dma((2, nh)),
        dma((nh,)),
        dma((nh,)),
        dma((2, nh)),
        dma((2, nh)),
        dma((2, nh)),
        dma((2, 2, nh)),
        dma((2, nh)),
    ]
    pairs = 17 * 2 * nh
    outs = pl.pallas_call(
        functools.partial(kernel, rows, nh),
        out_shape=[jax.ShapeDtypeStruct((BLK, width), BF16)] * 3
        + [jax.ShapeDtypeStruct((CLEAN, width), BF16)] * 2,
        in_specs=[hbm] * 9,
        out_specs=[hbm] * 5,
        scratch_shapes=scratch,
        compiler_params=pltpu.CompilerParams(
            collective_id=0, has_side_effects=True, vmem_limit_bytes=60 * 2**20
        ),
        cost_estimate=pl.CostEstimate(
            flops=pairs * 10 * BLK * BLK * HD,
            bytes_accessed=15 * 2**20,
            transcendentals=pairs * BLK * BLK,
        ),
        name="block_attention_backward",
    )(q_noised, dout, k_noised, v_noised, k_clean, v_clean, lse, delta, listed)
    return pl.pallas_call(
        copy_out,
        out_shape=[jax.ShapeDtypeStruct(out.shape, out.dtype) for out in outs],
        in_specs=[hbm] * 5,
        out_specs=[hbm] * 5,
        scratch_shapes=[vm(out.shape, out.dtype) for out in outs] + [dma((5,)), dma((5,))],
        name="copy_out",
    )(*outs)


def solution(mesh):
    rows = mesh.shape["ctx"] // (2 * RING)
    split = P("ctx", None)
    return jax.shard_map(
        functools.partial(per_device, rows),
        mesh=mesh,
        in_specs=(split,) * 4 + (P(None, "ctx"),) * 2 + (split,) * 3,
        out_specs=(split,) * 5,
        check_vma=False,
    )
```
